32 devices in a mesh: row: 4 (over y, core), col: 8 (over z, x).
Axes of the slice: x: 2, y: 2, z: 4, core: 2. Of those that a mesh axis runs over, the one named last changes fastest.
Arguments:
- volts: bfloat16 [2, 512, 4096], P(None, ('row', 'col')), may hold values from -6 to 6
- pattern: int32 [32, 32], replicated, may hold values from -1 to 62, as said below
- owner_slot: int32 [64], replicated, may hold values from 0 to 63, each once
Outputs:
- stacks: float32 [64, 4, 255], P(('row', 'col'))
The draws below stay inside these ranges and needn't reach their ends.
Inputs may be any that keep to these rules, and one draw needn't show every extreme that they name: pattern[p, q] is either q - p + 31 or -1; it is -1 where p == q. `owner_slot`: a permutation.
All inputs are finite; a program needn't handle non-finite values.
Results may differ from the reference program's by a relative error of at most 0.0003.
Values may be sent and summed in bfloat16 or wider, within the bound.
A program may use at most 64 MiB of HBM per device.

```python
import jax
import jax.numpy as jnp
from jax import lax

GRID_COLUMNS = 128
CHAN = 2
TIME_SAMPLES = 256
GR = 32
ANTENNA_COUNT = 4096
CHANNEL_SAMPLES = 512
NSTACK = 64
KSEP = 255


def draw_pattern(key, part):
    key = jax.random.fold_in(key, 7)
    first = jnp.arange(GR, dtype=jnp.int32)[:, None]
    second = jnp.arange(GR, dtype=jnp.int32)[None, :]
    flagged = jax.random.randint(key, (GR, GR), 0, 8) == 0
    corner = (first == 0) & (second == GR - 1)
    keep = (jnp.logical_not(flagged) | corner) & (first != second)
    return jnp.where(keep, second - first + GR - 1, -1).astype(jnp.int32)


def steps_of(key, extent, shards, least, top_value):
    gain = 1.0
    for position, blocks in shards:
        steps = jax.random.uniform(jax.random.fold_in(jax.random.fold_in(key, 6), position), (blocks,), jnp.float32, least / len(shards), top_value / len(shards))
        gain = gain * jnp.repeat(jnp.exp(steps), extent[position] // blocks).reshape((-1,) + (1,) * (len(extent) - 1 - position))
    return gain


def centred(key, extent, deviation, limit, split=(), kind=jnp.bfloat16):
    result = jax.random.normal(key, extent, jnp.float32) * deviation
    if len(split) > 0:
        result = steps_of(key, extent, split, -0.22, 0.18) * result
    return jnp.clip(result, min=-limit, max=limit).astype(kind)


def setup_inputs(seed: int = 0) -> dict:
    key_of = jax.random.split(jax.random.key(seed), 4)
    return {
        "volts": centred(key_of[0], (2, CHANNEL_SAMPLES, ANTENNA_COUNT), 1.0, 6.0, ((1, 32),)),
        "pattern": draw_pattern(jax.random.fold_in(key_of[3], 71), 0),
        "owner_slot": jax.random.permutation(key_of[2], NSTACK).astype(jnp.int32),
    }


def fold_diagonals(blocks):
    width = blocks.shape[-1]
    lead = blocks.shape[:-2]
    flipped = blocks[..., ::-1, :]
    padded = jnp.pad(flipped, [(0, 0)] * (blocks.ndim - 1) + [(0, width)])
    flat = padded.reshape(lead + (2 * width * width,))[..., :width * (2 * width - 1)]
    return flat.reshape(lead + (width, 2 * width - 1)).sum(axis=-2)

def reference(volts, pattern, owner_slot):
    voltages = volts.astype(jnp.float32).reshape(2, CHAN, TIME_SAMPLES, GR, GRID_COLUMNS)
    rotated = jnp.stack([-voltages[1], voltages[0]])
    highest = lax.Precision.HIGHEST

    def row_step(totals, grid_row):
        current = lax.dynamic_index_in_dim(voltages, grid_row, 3, keepdims=False)
        real_part = jnp.einsum('xcta,xctqb->cqab', current, voltages, precision=highest)
        imag_part = jnp.einsum('xcta,xctqb->cqab', current, rotated, precision=highest)
        folded = fold_diagonals(jnp.stack([real_part, imag_part], axis=1))
        folded = folded.transpose(2, 0, 1, 3).reshape(GR, 2 * CHAN, KSEP)
        keys = lax.dynamic_index_in_dim(pattern, grid_row, 0, keepdims=False)
        segment = jnp.where(keys >= 0, keys, NSTACK).astype(jnp.int32)
        summed = jax.ops.segment_sum(folded, segment, NSTACK + 1)[:NSTACK]
        return (totals + summed, None)
    start = jnp.zeros((NSTACK, 2 * CHAN, KSEP), jnp.float32)
    totals, unused = lax.scan(row_step, start, jnp.arange(GR, dtype=jnp.int32))
    flat_keys = pattern.reshape(-1)
    segment = jnp.where(flat_keys >= 0, flat_keys, NSTACK).astype(jnp.int32)
    pair_counts = jax.ops.segment_sum(jnp.ones(flat_keys.shape, jnp.float32), segment, NSTACK + 1)[:NSTACK]
    separation_offsets = jnp.abs(jnp.arange(KSEP, dtype=jnp.float32) - (GRID_COLUMNS - 1.0))
    antenna_pairs = pair_counts[:, None] * (GRID_COLUMNS - separation_offsets)[None, :]
    stack_scale = 1.0 / jnp.sqrt(2.0 * TIME_SAMPLES * jnp.maximum(antenna_pairs, 1.0))
    normed = totals * stack_scale[:, None, :]
    return jnp.zeros_like(normed).at[owner_slot].set(normed)
```

```python
import functools

import jax
import jax.numpy as jnp
from jax import lax
from jax.experimental import pallas as pl
from jax.experimental.pallas import tpu as pltpu
from jax.sharding import PartitionSpec as P

GRID_COLUMNS = 128
CHAN = 2
TIME_SAMPLES = 256
DEPTH = 256
MESH = pl.DeviceIdType.MESH


def iota(shape, dim):
    return lax.broadcasted_iota(jnp.int32, shape, dim)


def one_hot(condition):
    return jnp.where(condition, 1.0, 0.0).astype(jnp.bfloat16)


def dot(a, b, contract=((1,), (0,))):
    return lax.dot_general(a, b, (contract, ((), ())), preferred_element_type=jnp.float32)


def split3(x):
    high = x.astype(jnp.bfloat16)
    rest = x - high.astype(jnp.float32)
    middle = rest.astype(jnp.bfloat16)
    low = (rest - middle.astype(jnp.float32)).astype(jnp.bfloat16)
    return high, middle, low


def kernel(row_count, col_count, volts_ref, pattern_ref, owner_ref, out_ref,
           rhs_ref, lhs_ref, mask_ref, acc_ref, send_ref, recv_ref, send_sem, recv_sem):
    device_count = row_count * col_count
    grid_rows = pattern_ref.shape[0]
    samples = volts_ref.shape[1]
    unit = 2 * samples
    total = grid_rows * unit
    width = GRID_COLUMNS
    stack_count = owner_ref.shape[1]
    mask_width = mask_ref.shape[1]
    me = lax.axis_index("row") * col_count + lax.axis_index("col")

    barrier = pltpu.get_barrier_semaphore()

    def greet(step, carry):
        other = lax.rem(me + step, device_count)
        pl.semaphore_signal(barrier, inc=1, device_id=(other // col_count, lax.rem(other, col_count)),
                            device_id_type=MESH)
        return carry

    lax.fori_loop(1, device_count, greet, 0)

    store = rhs_ref.dtype
    for p in range(grid_rows):
        real = volts_ref[0, :, p * width:(p + 1) * width].astype(store)
        imag = volts_ref[1, :, p * width:(p + 1) * width].astype(store)
        start = p * unit
        rhs_ref[start:start + samples, :width] = real
        rhs_ref[start + samples:start + unit, :width] = imag
        rhs_ref[start:start + samples, width:] = -imag
        rhs_ref[start + samples:start + unit, width:] = real
    rhs_ref[total:, :] = jnp.zeros((DEPTH, 2 * width), store)

    flip = one_hot(iota((width, width), 0) + iota((width, width), 1) == width - 1)
    for block in range(total // DEPTH):
        rows = rhs_ref[block * DEPTH:(block + 1) * DEPTH, :width].astype(jnp.bfloat16)
        lhs_ref[:, block * DEPTH:(block + 1) * DEPTH] = dot(flip, rows, ((1,), (1,))).astype(jnp.bfloat16)

    valid = one_hot(pattern_ref[...] >= 0)
    flip_rows = one_hot(iota((grid_rows, grid_rows), 0) + iota((grid_rows, grid_rows), 1) == grid_rows - 1)
    widen = one_hot(iota((grid_rows, mask_width), 0) == iota((grid_rows, mask_width), 1))
    spread = one_hot(iota((grid_rows, total), 1) // unit == grid_rows - 1 - iota((grid_rows, total), 0))
    count = None
    for sign, contract in enumerate((((1,), (0,)), ((1,), (1,)))):
        turned = dot(flip_rows, valid, contract).astype(jnp.bfloat16)
        skewed = pltpu.roll(dot(turned, widen), 0, 1, stride=1, stride_axis=0).T.astype(jnp.bfloat16)
        mask_ref[sign] = dot(skewed, spread)
        if sign == 0:
            count = dot(skewed, jnp.ones((grid_rows, width), jnp.bfloat16))[:stack_count]

    no_pairs = jnp.zeros((8, 2 * width), jnp.float32)
    for part in range(2):
        acc_ref[part, grid_rows - 1] = no_pairs
        acc_ref[part, stack_count - 1] = no_pairs

    unwrapped = iota((width, width), 1) >= iota((width, width), 0)

    def one_difference(depth, d, carry):
        row = pl.ds(grid_rows - 1 + d, 1)
        left = lhs_ref[:, :depth]
        left = jnp.concatenate(
            [left * mask_ref[sign, row, :depth].astype(jnp.bfloat16) for sign in range(2)], axis=0
        )
        right = rhs_ref[pl.ds(pl.multiple_of(d * unit, unit), depth), :].astype(jnp.bfloat16)
        gram = dot(left, right)
        for sign in range(2):
            k = grid_rows - 1 + d if sign == 0 else grid_rows - 1 - d
            for part in range(2):
                tile = gram[sign * width:(sign + 1) * width, part * width:(part + 1) * width]
                tile = pltpu.roll(tile, 0, 1, stride=1, stride_axis=0)
                first = jnp.where(unwrapped, tile, 0.0).reshape(width // 8, 8, width)
                second = jnp.where(unwrapped, 0.0, tile).reshape(width // 8, 8, width)
                acc_ref[part, k, :, :width] = jnp.sum(first, axis=0)
                acc_ref[part, k, :, width:] = jnp.sum(second, axis=0)
        return carry

    per_block = DEPTH // unit
    for blocks in range(total // DEPTH, 0, -1):
        begin = max(1, grid_rows - blocks * per_block)
        end = grid_rows - (blocks - 1) * per_block
        lax.fori_loop(begin, end, functools.partial(one_difference, blocks * DEPTH), 0)

    lanes = 2 * width
    reverse = one_hot(iota((lanes, lanes), 0) + iota((lanes, lanes), 1) == lanes - 2)
    offsets = jnp.abs(iota((stack_count, lanes), 1) - (width - 1)).astype(jnp.float32)
    pairs = jnp.concatenate([count, count], axis=1) * (width - offsets)
    scale = 1.0 / jnp.sqrt(2.0 * TIME_SAMPLES * jnp.maximum(pairs, 1.0))
    parts = []
    for part in range(2):
        folded = jnp.sum(acc_ref[part], axis=1)
        behind = sum(dot(piece, reverse) for piece in split3(folded[:grid_rows]))
        if part == 1:
            behind = -behind
        parts.append(jnp.concatenate([behind, folded[grid_rows:]], axis=0) * scale)
    stacked = jnp.concatenate(parts, axis=1)

    send_rows = device_count * 8
    index = iota((send_rows, stack_count), 0)
    wanted = one_hot(index // 4 == owner_ref[...])
    picked = sum(dot(wanted, piece) for piece in split3(stacked))
    quarter = iota((send_rows, width), 0) % 4
    blocks = picked[:, 3 * width:]
    for m in range(3):
        blocks = jnp.where(quarter == m, picked[:, m * width:(m + 1) * width], blocks)
    send_ref[...] = blocks.reshape(device_count, 8, width)

    pl.semaphore_wait(barrier, device_count - 1)

    def send(step, carry):
        other = lax.rem(me + step, device_count)
        pltpu.make_async_remote_copy(
            src_ref=send_ref.at[other], dst_ref=recv_ref.at[me], send_sem=send_sem, recv_sem=recv_sem,
            device_id=(other // col_count, lax.rem(other, col_count)), device_id_type=MESH,
        ).start()
        return carry

    lax.fori_loop(1, device_count, send, 0)
    recv_ref[me] = send_ref[me]
    others = pl.ds(0, device_count - 1)
    pltpu.make_async_copy(recv_ref.at[others], recv_ref.at[others], recv_sem).wait()
    half = device_count // CHAN
    for chan in range(CHAN):
        owned = jnp.sum(recv_ref[chan * half:(chan + 1) * half], axis=0)
        for slot in range(2):
            for part in range(2):
                line = slot * 4 + part * 2
                out_ref[slot, chan * 2 + part, :width] = owned[line]
                out_ref[slot, chan * 2 + part, width:] = owned[line + 1, :width - 1]
    pltpu.make_async_copy(send_ref.at[others], send_ref.at[others], send_sem).wait()


def per_device(volts, pattern, owner_slot):
    row_count = lax.axis_size("row")
    col_count = lax.axis_size("col")
    device_count = row_count * col_count
    grid_rows = pattern.shape[0]
    stack_count = owner_slot.shape[0]
    samples = volts.shape[1]
    total = grid_rows * 2 * samples
    store = jnp.bfloat16 if samples % 16 == 0 else jnp.float32
    mask_width = -(-stack_count // 128) * 128
    vmem = pl.BlockSpec(memory_space=pltpu.VMEM)
    return pl.pallas_call(
        functools.partial(kernel, row_count, col_count),
        out_shape=jax.ShapeDtypeStruct(
            (stack_count // device_count, 2 * CHAN, 2 * GRID_COLUMNS - 1), jnp.float32),
        in_specs=[vmem] * 3,
        out_specs=vmem,
        scratch_shapes=[
            pltpu.VMEM((total + DEPTH, 2 * GRID_COLUMNS), store),
            pltpu.VMEM((GRID_COLUMNS, total), jnp.bfloat16),
            pltpu.VMEM((2, mask_width, total), jnp.float32),
            pltpu.VMEM((2, stack_count, 8, 2 * GRID_COLUMNS), jnp.float32),
            pltpu.VMEM((device_count, 8, GRID_COLUMNS), jnp.float32),
            pltpu.VMEM((device_count, 8, GRID_COLUMNS), jnp.float32),
            pltpu.SemaphoreType.DMA,
            pltpu.SemaphoreType.DMA,
        ],
        compiler_params=pltpu.CompilerParams(
            collective_id=0, has_side_effects=True, vmem_limit_bytes=48 * 1024 * 1024),
        cost_estimate=pl.CostEstimate(flops=2 * 256 * 256 * 19456, bytes_accessed=1 << 20, transcendentals=0),
    )(volts, pattern, owner_slot.reshape(1, stack_count))


def solution(mesh):
    return jax.shard_map(
        per_device,
        mesh=mesh,
        in_specs=(P(None, ("row", "col"), None), P(), P()),
        out_specs=P(("row", "col"), None, None),
        check_vma=False,
    )
```

```python
import functools

import jax
import jax.numpy as jnp
from jax import lax
from jax.experimental import pallas as pl
from jax.experimental.pallas import tpu as pltpu
from jax.sharding import PartitionSpec as P

GRID_COLUMNS = 128
CHAN = 2
TIME_SAMPLES = 256
DEPTH = 256
UNROLL = 4
MESH = pl.DeviceIdType.MESH


def iota(shape, dim):
    return lax.broadcasted_iota(jnp.int32, shape, dim)


def one_hot(condition):
    return jnp.where(condition, 1.0, 0.0).astype(jnp.bfloat16)


def dot(a, b, contract=((1,), (0,))):
    return lax.dot_general(a, b, (contract, ((), ())), preferred_element_type=jnp.float32)


def split3(x):
    high = x.astype(jnp.bfloat16)
    rest = x - high.astype(jnp.float32)
    middle = rest.astype(jnp.bfloat16)
    low = (rest - middle.astype(jnp.float32)).astype(jnp.bfloat16)
    return high, middle, low


def kernel(row_count, col_count, volts_hbm, pattern_hbm, owner_hbm, out_ref,
           volts_ref, pattern_ref, owner_ref, rhs_ref, lhs_ref, mask_ref, scale_ref, wanted_ref, sum_ref,
           send_ref, recv_ref, load_sems, send_sem, recv_sem):
    device_count = row_count * col_count
    grid_rows = pattern_ref.shape[0]
    samples = volts_ref.shape[1]
    unit = 2 * samples
    total = grid_rows * unit
    width = GRID_COLUMNS
    lanes = 2 * width
    stack_count = owner_ref.shape[1]
    mask_width = -(-stack_count // 128) * 128
    me = lax.axis_index("row") * col_count + lax.axis_index("col")

    def place(device):
        return (device // col_count, lax.rem(device, col_count))

    loads = [
        pltpu.make_async_copy(source, target, load_sems.at[n])
        for n, (source, target) in enumerate(
            ((pattern_hbm, pattern_ref), (owner_hbm, owner_ref), (volts_hbm, volts_ref)))
    ]
    for load in loads:
        load.start()

    barrier = pltpu.get_barrier_semaphore()

    def greet(step, carry):
        other = lax.rem(me + step, device_count)
        pl.semaphore_signal(barrier, inc=1, device_id=place(other), device_id_type=MESH)
        return carry

    lax.fori_loop(1, device_count, greet, 0)

    loads[0].wait()
    valid = one_hot(pattern_ref[...] >= 0)
    flip_rows = one_hot(iota((grid_rows, grid_rows), 0) + iota((grid_rows, grid_rows), 1) == grid_rows - 1)
    widen = one_hot(iota((grid_rows, mask_width), 0) == iota((grid_rows, mask_width), 1))
    spread = one_hot(iota((grid_rows, total), 1) // unit == grid_rows - 1 - iota((grid_rows, total), 0))
    for sign, contract in enumerate((((1,), (0,)), ((1,), (1,)))):
        turned = dot(dot(flip_rows, valid, contract).astype(jnp.bfloat16), widen)
        skewed = pltpu.roll(turned, mask_width - (grid_rows - 1), 1, stride=1, stride_axis=0)
        mask_ref[sign] = dot(skewed.T.astype(jnp.bfloat16)[:grid_rows], spread)
        if sign == 0:
            by_stack = pltpu.roll(turned, 0, 1, stride=1, stride_axis=0).T.astype(jnp.bfloat16)
            count = dot(by_stack, jnp.ones((grid_rows, lanes), jnp.bfloat16))[:stack_count]
            offsets = jnp.abs(iota((stack_count, lanes), 1) - (width - 1)).astype(jnp.float32)
            pairs = jnp.maximum(count * (width - offsets), 1.0)
            scale_ref[...] = 1.0 / jnp.sqrt(2.0 * TIME_SAMPLES * pairs)

    loads[1].wait()
    send_rows = device_count * 8
    owner = owner_ref[...]
    owner = jnp.concatenate([owner, owner, owner], axis=1)
    wanted_ref[...] = one_hot(iota((send_rows, 3 * stack_count), 0) // 4 == owner)

    rhs_ref[total:, :] = jnp.zeros((DEPTH, lanes), rhs_ref.dtype)
    sum_ref[:, stack_count - 8:, :] = jnp.zeros((4, 8, width), jnp.float32)

    loads[2].wait()
    store = rhs_ref.dtype
    for p in range(grid_rows):
        real = volts_ref[0, :, p * width:(p + 1) * width].astype(store)
        imag = volts_ref[1, :, p * width:(p + 1) * width].astype(store)
        start = p * unit
        rhs_ref[start:start + samples, :width] = real
        rhs_ref[start + samples:start + unit, :width] = imag
        rhs_ref[start:start + samples, width:] = -imag
        rhs_ref[start + samples:start + unit, width:] = real

    flip = one_hot(iota((width, width), 0) + iota((width, width), 1) == width - 1)
    for block in range(total // DEPTH):
        rows = rhs_ref[block * DEPTH:(block + 1) * DEPTH, :width].astype(jnp.bfloat16)
        lhs_ref[:, block * DEPTH:(block + 1) * DEPTH] = dot(flip, rows, ((1,), (1,))).astype(jnp.bfloat16)

    unwrapped = iota((width, width), 1) >= iota((width, width), 0)

    def one_difference(depth, d, carry):
        left = lhs_ref[:, :depth]
        left = jnp.concatenate(
            [left * mask_ref[sign, pl.ds(d, 1), :depth].astype(jnp.bfloat16) for sign in range(2)], axis=0
        )
        right = rhs_ref[pl.ds(pl.multiple_of(d * unit, unit), depth), :].astype(jnp.bfloat16)
        gram = dot(left, right)
        for sign in range(2):
            k = grid_rows - 1 + d if sign == 0 else grid_rows - 1 - d
            for part in range(2):
                tile = gram[sign * width:(sign + 1) * width, part * width:(part + 1) * width]
                tile = pltpu.roll(tile, 0, 1, stride=1, stride_axis=0)
                first = jnp.where(unwrapped, tile, 0.0)
                second = jnp.where(unwrapped, 0.0, tile)
                sum_ref[2 * part, pl.ds(k, 1), :] = jnp.sum(first, axis=0, keepdims=True)
                sum_ref[2 * part + 1, pl.ds(k, 1), :] = jnp.sum(second, axis=0, keepdims=True)
        return carry

    per_block = DEPTH // unit
    for blocks in range(total // DEPTH, 0, -1):
        lax.fori_loop(
            grid_rows - blocks * per_block, grid_rows - (blocks - 1) * per_block,
            functools.partial(one_difference, blocks * DEPTH), 0, unroll=UNROLL)

    reverse = one_hot(iota((lanes, lanes), 0) + iota((lanes, lanes), 1) == lanes - 2)
    folded = [jnp.concatenate([sum_ref[2 * part], sum_ref[2 * part + 1]], axis=1) for part in range(2)]
    behind = jnp.concatenate([folded[part][:grid_rows] for part in range(2)], axis=0)
    behind = dot(jnp.concatenate(split3(behind), axis=0), reverse)
    behind = sum(behind[n * 2 * grid_rows:(n + 1) * 2 * grid_rows] for n in range(3))
    scale = scale_ref[...]
    real = jnp.concatenate([behind[:grid_rows], folded[0][grid_rows:]], axis=0) * scale
    imag = jnp.concatenate([-behind[grid_rows:], folded[1][grid_rows:]], axis=0) * scale
    stacked = jnp.concatenate([real, imag], axis=1)
    picked = dot(wanted_ref[...], jnp.concatenate(split3(stacked), axis=0))
    quarter = iota((send_rows, width), 0) % 4
    blocks = picked[:, 3 * width:]
    for m in range(3):
        blocks = jnp.where(quarter == m, picked[:, m * width:(m + 1) * width], blocks)
    send_ref[...] = blocks.reshape(device_count, 8, width)

    pl.semaphore_wait(barrier, device_count - 1)

    def send(step, carry):
        other = lax.rem(me + step, device_count)
        pltpu.make_async_remote_copy(
            src_ref=send_ref.at[other], dst_ref=recv_ref.at[me], send_sem=send_sem, recv_sem=recv_sem,
            device_id=place(other), device_id_type=MESH,
        ).start()
        return carry

    lax.fori_loop(1, device_count, send, 0)
    recv_ref[me] = send_ref[me]
    others = pl.ds(0, device_count - 1)
    pltpu.make_async_copy(recv_ref.at[others], recv_ref.at[others], recv_sem).wait()
    half = device_count // CHAN
    for chan in range(CHAN):
        owned = jnp.sum(recv_ref[chan * half:(chan + 1) * half], axis=0)
        for slot in range(2):
            for part in range(2):
                line = slot * 4 + part * 2
                out_ref[slot, chan * 2 + part, :width] = owned[line]
                out_ref[slot, chan * 2 + part, width:] = owned[line + 1, :width - 1]
    pltpu.make_async_copy(send_ref.at[others], send_ref.at[others], send_sem).wait()


def per_device(volts, pattern, owner_slot):
    row_count = lax.axis_size("row")
    col_count = lax.axis_size("col")
    device_count = row_count * col_count
    grid_rows = pattern.shape[0]
    stack_count = owner_slot.shape[0]
    samples = volts.shape[1]
    total = grid_rows * 2 * samples
    store = jnp.bfloat16 if samples % 16 == 0 else jnp.float32
    vmem = pl.BlockSpec(memory_space=pltpu.VMEM)
    return pl.pallas_call(
        functools.partial(kernel, row_count, col_count),
        out_shape=jax.ShapeDtypeStruct(
            (stack_count // device_count, 2 * CHAN, 2 * GRID_COLUMNS - 1), jnp.float32),
        in_specs=[pl.BlockSpec(memory_space=pltpu.HBM)] * 3,
        out_specs=vmem,
        scratch_shapes=[
            pltpu.VMEM(volts.shape, volts.dtype),
            pltpu.VMEM(pattern.shape, pattern.dtype),
            pltpu.VMEM((1, stack_count), owner_slot.dtype),
            pltpu.VMEM((total + DEPTH, 2 * GRID_COLUMNS), store),
            pltpu.VMEM((GRID_COLUMNS, total), jnp.bfloat16),
            pltpu.VMEM((2, grid_rows, total), jnp.float32),
            pltpu.VMEM((stack_count, 2 * GRID_COLUMNS), jnp.float32),
            pltpu.VMEM((device_count * 8, 3 * stack_count), jnp.bfloat16),
            pltpu.VMEM((4, stack_count, GRID_COLUMNS), jnp.float32),
            pltpu.VMEM((device_count, 8, GRID_COLUMNS), jnp.float32),
            pltpu.VMEM((device_count, 8, GRID_COLUMNS), jnp.float32),
            pltpu.SemaphoreType.DMA((3,)),
            pltpu.SemaphoreType.DMA,
            pltpu.SemaphoreType.DMA,
        ],
        compiler_params=pltpu.CompilerParams(
            collective_id=0, has_side_effects=True, vmem_limit_bytes=48 * 1024 * 1024),
        cost_estimate=pl.CostEstimate(flops=2 * 256 * 256 * 19456, bytes_accessed=1 << 20, transcendentals=0),
    )(volts, pattern, owner_slot.reshape(1, stack_count))


def solution(mesh):
    return jax.shard_map(
        per_device,
        mesh=mesh,
        in_specs=(P(None, ("row", "col"), None), P(), P()),
        out_specs=P(("row", "col"), None, None),
        check_vma=False,
    )
```

```python
import functools

import jax
import jax.numpy as jnp
from jax import lax
from jax.experimental import pallas as pl
from jax.experimental.pallas import tpu as pltpu
from jax.sharding import PartitionSpec as P

GRID_COLUMNS = 128
CHAN = 2
TIME_SAMPLES = 256
DEPTH = 256
UNROLL = 8
MESH = pl.DeviceIdType.MESH


def iota(shape, dim):
    return lax.broadcasted_iota(jnp.int32, shape, dim)


def one_hot(condition):
    return jnp.where(condition, 1.0, 0.0).astype(jnp.bfloat16)


def dot(a, b, contract=((1,), (0,))):
    return lax.dot_general(a, b, (contract, ((), ())), preferred_element_type=jnp.float32)


def split3(x):
    high = x.astype(jnp.bfloat16)
    rest = x - high.astype(jnp.float32)
    middle = rest.astype(jnp.bfloat16)
    low = (rest - middle.astype(jnp.float32)).astype(jnp.bfloat16)
    return high, middle, low


def kernel(row_count, col_count, volts_hbm, pattern_hbm, owner_hbm, out_ref,
           volts_ref, pattern_ref, owner_ref, rhs_ref, lhs_ref, mask_ref, scale_ref, wanted_ref, sum_ref,
           send_ref, recv_ref, load_sems, send_sem, recv_sem):
    device_count = row_count * col_count
    grid_rows = pattern_ref.shape[0]
    samples = volts_ref.shape[1]
    unit = 2 * samples
    total = grid_rows * unit
    width = GRID_COLUMNS
    lanes = 2 * width
    stack_count = owner_ref.shape[1]
    mask_width = -(-stack_count // 128) * 128
    me = lax.axis_index("row") * col_count + lax.axis_index("col")

    def place(device):
        return (device // col_count, lax.rem(device, col_count))

    loads = [
        pltpu.make_async_copy(source, target, load_sems.at[n])
        for n, (source, target) in enumerate(
            ((pattern_hbm, pattern_ref), (owner_hbm, owner_ref), (volts_hbm, volts_ref)))
    ]
    for load in loads:
        load.start()

    barrier = pltpu.get_barrier_semaphore()

    def greet(step, carry):
        other = lax.rem(me + step, device_count)
        pl.semaphore_signal(barrier, inc=1, device_id=place(other), device_id_type=MESH)
        return carry

    lax.fori_loop(1, device_count, greet, 0, unroll=device_count <= 32)

    loads[0].wait()
    valid = one_hot(pattern_ref[...] >= 0)
    flip_rows = one_hot(iota((grid_rows, grid_rows), 0) + iota((grid_rows, grid_rows), 1) == grid_rows - 1)
    widen = one_hot(iota((grid_rows, mask_width), 0) == iota((grid_rows, mask_width), 1))
    spread = one_hot(iota((grid_rows, total), 1) // unit == grid_rows - 1 - iota((grid_rows, total), 0))
    for sign, contract in enumerate((((1,), (0,)), ((1,), (1,)))):
        turned = dot(dot(flip_rows, valid, contract).astype(jnp.bfloat16), widen)
        skewed = pltpu.roll(turned, mask_width - (grid_rows - 1), 1, stride=1, stride_axis=0)
        mask_ref[sign] = dot(skewed.T.astype(jnp.bfloat16)[:grid_rows], spread)
        if sign == 0:
            by_stack = pltpu.roll(turned, 0, 1, stride=1, stride_axis=0).T.astype(jnp.bfloat16)
            count = dot(by_stack, jnp.ones((grid_rows, lanes), jnp.bfloat16))[:stack_count]
            offsets = jnp.abs(iota((stack_count, lanes), 1) - (width - 1)).astype(jnp.float32)
            pairs = jnp.maximum(count * (width - offsets), 1.0)
            scale_ref[...] = 1.0 / jnp.sqrt(2.0 * TIME_SAMPLES * pairs)

    loads[1].wait()
    send_rows = device_count * 8
    owner = owner_ref[...]
    owner = jnp.concatenate([owner, owner, owner], axis=1)
    wanted_ref[...] = one_hot(iota((send_rows, 3 * stack_count), 0) // 4 == owner)

    rhs_ref[total:, :] = jnp.zeros((DEPTH, lanes), rhs_ref.dtype)
    sum_ref[:, stack_count - 8:, :] = jnp.zeros((4, 8, width), jnp.float32)

    loads[2].wait()
    store = rhs_ref.dtype
    for p in range(grid_rows):
        real = volts_ref[0, :, p * width:(p + 1) * width].astype(store)
        imag = volts_ref[1, :, p * width:(p + 1) * width].astype(store)
        start = p * unit
        rhs_ref[start:start + samples, :width] = real
        rhs_ref[start + samples:start + unit, :width] = imag
        rhs_ref[start:start + samples, width:] = -imag
        rhs_ref[start + samples:start + unit, width:] = real

    flip = one_hot(iota((width, width), 0) + iota((width, width), 1) == width - 1)
    for block in range(total // DEPTH):
        rows = rhs_ref[block * DEPTH:(block + 1) * DEPTH, :width].astype(jnp.bfloat16)
        lhs_ref[:, block * DEPTH:(block + 1) * DEPTH] = dot(flip, rows, ((1,), (1,))).astype(jnp.bfloat16)

    unwrapped = iota((width, width), 1) >= iota((width, width), 0)

    def one_difference(depth, d, carry):
        left = lhs_ref[:, :depth]
        left = jnp.concatenate(
            [left * mask_ref[sign, pl.ds(d, 1), :depth].astype(jnp.bfloat16) for sign in range(2)], axis=0
        )
        right = rhs_ref[pl.ds(pl.multiple_of(d * unit, unit), depth), :].astype(jnp.bfloat16)
        gram = dot(left, right)
        for sign in range(2):
            k = grid_rows - 1 + d if sign == 0 else grid_rows - 1 - d
            for part in range(2):
                tile = gram[sign * width:(sign + 1) * width, part * width:(part + 1) * width]
                tile = pltpu.roll(tile, 0, 1, stride=1, stride_axis=0)
                first = jnp.where(unwrapped, tile, 0.0)
                second = jnp.where(unwrapped, 0.0, tile)
                sum_ref[2 * part, pl.ds(k, 1), :] = jnp.sum(first, axis=0, keepdims=True)
                sum_ref[2 * part + 1, pl.ds(k, 1), :] = jnp.sum(second, axis=0, keepdims=True)
        return carry

    per_block = DEPTH // unit
    for blocks in range(total // DEPTH, 0, -1):
        lax.fori_loop(
            grid_rows - blocks * per_block, grid_rows - (blocks - 1) * per_block,
            functools.partial(one_difference, blocks * DEPTH), 0, unroll=UNROLL)

    reverse = one_hot(iota((lanes, lanes), 0) + iota((lanes, lanes), 1) == lanes - 2)
    folded = [jnp.concatenate([sum_ref[2 * part], sum_ref[2 * part + 1]], axis=1) for part in range(2)]
    behind = jnp.concatenate([folded[part][:grid_rows] for part in range(2)], axis=0)
    behind = dot(jnp.concatenate(split3(behind), axis=0), reverse)
    behind = sum(behind[n * 2 * grid_rows:(n + 1) * 2 * grid_rows] for n in range(3))
    scale = scale_ref[...]
    real = jnp.concatenate([behind[:grid_rows], folded[0][grid_rows:]], axis=0) * scale
    imag = jnp.concatenate([-behind[grid_rows:], folded[1][grid_rows:]], axis=0) * scale
    stacked = jnp.concatenate([real, imag], axis=1)
    picked = dot(wanted_ref[...], jnp.concatenate(split3(stacked), axis=0))
    quarter = iota((send_rows, width), 0) % 4
    blocks = picked[:, 3 * width:]
    for m in range(3):
        blocks = jnp.where(quarter == m, picked[:, m * width:(m + 1) * width], blocks)
    send_ref[...] = blocks.reshape(device_count, 8, width)

    pl.semaphore_wait(barrier, device_count - 1)

    def send(step, carry):
        other = lax.rem(me + step, device_count)
        pltpu.make_async_remote_copy(
            src_ref=send_ref.at[other], dst_ref=recv_ref.at[me], send_sem=send_sem, recv_sem=recv_sem,
            device_id=place(other), device_id_type=MESH,
        ).start()
        return carry

    lax.fori_loop(1, device_count, send, 0, unroll=device_count <= 32)
    recv_ref[me] = send_ref[me]
    others = pl.ds(0, device_count - 1)
    pltpu.make_async_copy(recv_ref.at[others], recv_ref.at[others], recv_sem).wait()
    half = device_count // CHAN
    for chan in range(CHAN):
        owned = jnp.sum(recv_ref[chan * half:(chan + 1) * half], axis=0)
        for slot in range(2):
            for part in range(2):
                line = slot * 4 + part * 2
                out_ref[slot, chan * 2 + part, :width] = owned[line]
                out_ref[slot, chan * 2 + part, width:] = owned[line + 1, :width - 1]
    pltpu.make_async_copy(send_ref.at[others], send_ref.at[others], send_sem).wait()


def per_device(volts, pattern, owner_slot):
    row_count = lax.axis_size("row")
    col_count = lax.axis_size("col")
    device_count = row_count * col_count
    grid_rows = pattern.shape[0]
    stack_count = owner_slot.shape[0]
    samples = volts.shape[1]
    total = grid_rows * 2 * samples
    store = jnp.bfloat16 if samples % 16 == 0 else jnp.float32
    vmem = pl.BlockSpec(memory_space=pltpu.VMEM)
    return pl.pallas_call(
        functools.partial(kernel, row_count, col_count),
        out_shape=jax.ShapeDtypeStruct(
            (stack_count // device_count, 2 * CHAN, 2 * GRID_COLUMNS - 1), jnp.float32),
        in_specs=[pl.BlockSpec(memory_space=pltpu.HBM)] * 3,
        out_specs=vmem,
        scratch_shapes=[
            pltpu.VMEM(volts.shape, volts.dtype),
            pltpu.VMEM(pattern.shape, pattern.dtype),
            pltpu.VMEM((1, stack_count), owner_slot.dtype),
            pltpu.VMEM((total + DEPTH, 2 * GRID_COLUMNS), store),
            pltpu.VMEM((GRID_COLUMNS, total), jnp.bfloat16),
            pltpu.VMEM((2, grid_rows, total), jnp.float32),
            pltpu.VMEM((stack_count, 2 * GRID_COLUMNS), jnp.float32),
            pltpu.VMEM((device_count * 8, 3 * stack_count), jnp.bfloat16),
            pltpu.VMEM((4, stack_count, GRID_COLUMNS), jnp.float32),
            pltpu.VMEM((device_count, 8, GRID_COLUMNS), jnp.float32),
            pltpu.VMEM((device_count, 8, GRID_COLUMNS), jnp.float32),
            pltpu.SemaphoreType.DMA((3,)),
            pltpu.SemaphoreType.DMA,
            pltpu.SemaphoreType.DMA,
        ],
        compiler_params=pltpu.CompilerParams(
            collective_id=0, has_side_effects=True, vmem_limit_bytes=60 * 1024 * 1024),
        cost_estimate=pl.CostEstimate(flops=2 * 256 * 256 * 19456, bytes_accessed=1 << 20, transcendentals=0),
    )(volts, pattern, owner_slot.reshape(1, stack_count))


def solution(mesh):
    return jax.shard_map(
        per_device,
        mesh=mesh,
        in_specs=(P(None, ("row", "col"), None), P(), P()),
        out_specs=P(("row", "col"), None, None),
        check_vma=False,
    )
```

```python
import functools

import jax
import jax.numpy as jnp
from jax import lax
from jax.experimental import pallas as pl
from jax.experimental.pallas import tpu as pltpu
from jax.sharding import PartitionSpec as P

GRID_COLUMNS = 128
CHAN = 2
TIME_SAMPLES = 256
DEPTH = 256
UNROLL = 8
MESH = pl.DeviceIdType.MESH


def iota(shape, dim):
    return lax.broadcasted_iota(jnp.int32, shape, dim)


def one_hot(condition):
    return jnp.where(condition, 1.0, 0.0).astype(jnp.bfloat16)


def dot(a, b, contract=((1,), (0,))):
    return lax.dot_general(a, b, (contract, ((), ())), preferred_element_type=jnp.float32)


def split3(x):
    high = x.astype(jnp.bfloat16)
    rest = x - high.astype(jnp.float32)
    middle = rest.astype(jnp.bfloat16)
    low = (rest - middle.astype(jnp.float32)).astype(jnp.bfloat16)
    return high, middle, low


def kernel(row_count, col_count, volts_hbm, pattern_hbm, owner_hbm, out_ref,
           volts_ref, pattern_ref, owner_ref, rhs_ref, lhs_ref, mask_ref, scale_ref, wanted_ref, sum_ref,
           send_ref, recv_ref, load_sems, send_sem, recv_sem):
    device_count = row_count * col_count
    grid_rows = pattern_ref.shape[0]
    samples = volts_ref.shape[1]
    unit = 2 * samples
    total = grid_rows * unit
    width = GRID_COLUMNS
    lanes = 2 * width
    stack_count = owner_ref.shape[1]
    mask_width = -(-stack_count // 128) * 128
    me = lax.axis_index("row") * col_count + lax.axis_index("col")

    def place(device):
        return (device // col_count, lax.rem(device, col_count))

    loads = [
        pltpu.make_async_copy(source, target, load_sems.at[n])
        for n, (source, target) in enumerate(
            ((pattern_hbm, pattern_ref), (owner_hbm, owner_ref), (volts_hbm, volts_ref)))
    ]
    for load in loads:
        load.start()

    barrier = pltpu.get_barrier_semaphore()

    def greet(step, carry):
        other = lax.rem(me + step, device_count)
        pl.semaphore_signal(barrier, inc=1, device_id=place(other), device_id_type=MESH)
        return carry

    lax.fori_loop(1, device_count, greet, 0, unroll=device_count <= 32)

    loads[0].wait()
    valid = jnp.where(pattern_ref[...] >= 0, 1.0, 0.0)
    flip_rows = one_hot(iota((grid_rows, grid_rows), 0) + iota((grid_rows, grid_rows), 1) == grid_rows - 1)
    more = mask_width - grid_rows
    widened = (
        jnp.concatenate([valid, jnp.zeros((grid_rows, more), valid.dtype)], axis=1),
        jnp.concatenate([valid, jnp.zeros((more, grid_rows), valid.dtype)], axis=0),
    )
    spread = one_hot(iota((grid_rows, total), 1) // unit == grid_rows - 1 - iota((grid_rows, total), 0))
    for sign, contract in enumerate((((1,), (0,)), ((1,), (1,)))):
        turned = dot(flip_rows, widened[sign].astype(jnp.bfloat16), contract)
        if sign == 0:
            unflipped = turned
        skewed = pltpu.roll(turned, mask_width - (grid_rows - 1), 1, stride=1, stride_axis=0)
        mask_ref[sign] = dot(skewed.T.astype(jnp.bfloat16)[:grid_rows], spread)

    rhs_ref[total:, :] = jnp.zeros((DEPTH, lanes), rhs_ref.dtype)
    sum_ref[:, stack_count - 8:, :] = jnp.zeros((4, 8, width), jnp.float32)

    loads[1].wait()
    loads[2].wait()
    store = rhs_ref.dtype
    for p in range(grid_rows):
        real = volts_ref[0, :, p * width:(p + 1) * width].astype(store)
        imag = volts_ref[1, :, p * width:(p + 1) * width].astype(store)
        start = p * unit
        rhs_ref[start:start + samples, :width] = real
        rhs_ref[start + samples:start + unit, :width] = imag
        rhs_ref[start:start + samples, width:] = -imag
        rhs_ref[start + samples:start + unit, width:] = real

    flip = one_hot(iota((width, width), 0) + iota((width, width), 1) == width - 1)
    for block in range(total // DEPTH):
        rows = rhs_ref[block * DEPTH:(block + 1) * DEPTH, :width].astype(jnp.bfloat16)
        lhs_ref[:, block * DEPTH:(block + 1) * DEPTH] = dot(flip, rows, ((1,), (1,))).astype(jnp.bfloat16)

    by_stack = pltpu.roll(unflipped, 0, 1, stride=1, stride_axis=0).T.astype(jnp.bfloat16)
    count = dot(by_stack, jnp.ones((grid_rows, lanes), jnp.bfloat16))[:stack_count]
    offsets = jnp.abs(iota((stack_count, lanes), 1) - (width - 1)).astype(jnp.float32)
    pairs = jnp.maximum(count * (width - offsets), 1.0)
    scale_ref[...] = 1.0 / jnp.sqrt(2.0 * TIME_SAMPLES * pairs)

    send_rows = device_count * 8
    owner = owner_ref[...]
    owner = jnp.concatenate([owner, owner, owner], axis=1)
    rows = iota((send_rows, 3 * stack_count), 0)
    slots = lax.rem(me + rows // 8, device_count) * 2 + rows // 4 % 2
    wanted_ref[...] = one_hot(slots == owner)

    unwrapped = iota((width, width), 1) >= iota((width, width), 0)

    def one_difference(depth, d, carry):
        left = lhs_ref[:, :depth].reshape(width // 16, 16, depth)
        masks = [
            jnp.broadcast_to(mask_ref[sign, pl.ds(d, 1), :depth], (16, depth)).astype(jnp.bfloat16)
            for sign in range(2)
        ]
        left = jnp.concatenate([(left * mask[None]).reshape(width, depth) for mask in masks], axis=0)
        right = rhs_ref[pl.ds(pl.multiple_of(d * unit, unit), depth), :].astype(jnp.bfloat16)
        gram = dot(left, right)
        for sign in range(2):
            k = grid_rows - 1 + d if sign == 0 else grid_rows - 1 - d
            for part in range(2):
                tile = gram[sign * width:(sign + 1) * width, part * width:(part + 1) * width]
                tile = pltpu.roll(tile, 0, 1, stride=1, stride_axis=0)
                first = jnp.where(unwrapped, tile, 0.0)
                second = jnp.where(unwrapped, 0.0, tile)
                sum_ref[2 * part, pl.ds(k, 1), :] = jnp.sum(first, axis=0, keepdims=True)
                sum_ref[2 * part + 1, pl.ds(k, 1), :] = jnp.sum(second, axis=0, keepdims=True)
        return carry

    per_block = DEPTH // unit
    for blocks in range(total // DEPTH, 0, -1):
        lax.fori_loop(
            grid_rows - blocks * per_block, grid_rows - (blocks - 1) * per_block,
            functools.partial(one_difference, blocks * DEPTH), 0, unroll=UNROLL)

    reverse = one_hot(iota((lanes, lanes), 0) + iota((lanes, lanes), 1) == lanes - 2)
    folded = [jnp.concatenate([sum_ref[2 * part], sum_ref[2 * part + 1]], axis=1) for part in range(2)]
    behind = jnp.concatenate([folded[part][:grid_rows] for part in range(2)], axis=0)
    behind = dot(jnp.concatenate(split3(behind), axis=0), reverse)
    behind = sum(behind[n * 2 * grid_rows:(n + 1) * 2 * grid_rows] for n in range(3))
    scale = scale_ref[...]
    real = jnp.concatenate([behind[:grid_rows], folded[0][grid_rows:]], axis=0) * scale
    imag = jnp.concatenate([-behind[grid_rows:], folded[1][grid_rows:]], axis=0) * scale
    stacked = jnp.concatenate([real, imag], axis=1)
    pieces = jnp.concatenate(split3(stacked), axis=0)

    def send(step, carry):
        pltpu.make_async_remote_copy(
            src_ref=send_ref.at[step], dst_ref=recv_ref.at[me], send_sem=send_sem, recv_sem=recv_sem,
            device_id=place(lax.rem(me + step, device_count)), device_id_type=MESH,
        ).start()
        return carry

    group = device_count // 4
    quarter = iota((group * 8, width), 0) % 4
    pl.semaphore_wait(barrier, device_count - 1)
    for first in range(0, device_count, group):
        picked = dot(wanted_ref[first * 8:(first + group) * 8, :], pieces)
        blocks = picked[:, 3 * width:]
        for m in range(3):
            blocks = jnp.where(quarter == m, picked[:, m * width:(m + 1) * width], blocks)
        send_ref[first:first + group] = blocks.reshape(group, 8, width)
        lax.fori_loop(max(first, 1), first + group, send, 0, unroll=device_count <= 32)
    recv_ref[me] = send_ref[0]
    others = pl.ds(0, device_count - 1)
    pltpu.make_async_copy(recv_ref.at[others], recv_ref.at[others], recv_sem).wait()
    half = device_count // CHAN
    for chan in range(CHAN):
        owned = jnp.sum(recv_ref[chan * half:(chan + 1) * half], axis=0)
        for slot in range(2):
            for part in range(2):
                line = slot * 4 + part * 2
                out_ref[slot, chan * 2 + part, :width] = owned[line]
                out_ref[slot, chan * 2 + part, width:] = owned[line + 1, :width - 1]
    pltpu.make_async_copy(send_ref.at[others], send_ref.at[others], send_sem).wait()


def per_device(volts, pattern, owner_slot):
    row_count = lax.axis_size("row")
    col_count = lax.axis_size("col")
    device_count = row_count * col_count
    grid_rows = pattern.shape[0]
    stack_count = owner_slot.shape[0]
    samples = volts.shape[1]
    total = grid_rows * 2 * samples
    store = jnp.bfloat16 if samples % 16 == 0 else jnp.float32
    vmem = pl.BlockSpec(memory_space=pltpu.VMEM)
    return pl.pallas_call(
        functools.partial(kernel, row_count, col_count),
        out_shape=jax.ShapeDtypeStruct(
            (stack_count // device_count, 2 * CHAN, 2 * GRID_COLUMNS - 1), jnp.float32),
        in_specs=[pl.BlockSpec(memory_space=pltpu.HBM)] * 3,
        out_specs=vmem,
        scratch_shapes=[
            pltpu.VMEM(volts.shape, volts.dtype),
            pltpu.VMEM(pattern.shape, pattern.dtype),
            pltpu.VMEM((1, stack_count), owner_slot.dtype),
            pltpu.VMEM((total + DEPTH, 2 * GRID_COLUMNS), store),
            pltpu.VMEM((GRID_COLUMNS, total), jnp.bfloat16),
            pltpu.VMEM((2, grid_rows, total), jnp.float32),
            pltpu.VMEM((stack_count, 2 * GRID_COLUMNS), jnp.float32),
            pltpu.VMEM((device_count * 8, 3 * stack_count), jnp.bfloat16),
            pltpu.VMEM((4, stack_count, GRID_COLUMNS), jnp.float32),
            pltpu.VMEM((device_count, 8, GRID_COLUMNS), jnp.float32),
            pltpu.VMEM((device_count, 8, GRID_COLUMNS), jnp.float32),
            pltpu.SemaphoreType.DMA((3,)),
            pltpu.SemaphoreType.DMA,
            pltpu.SemaphoreType.DMA,
        ],
        compiler_params=pltpu.CompilerParams(
            collective_id=0, has_side_effects=True, vmem_limit_bytes=60 * 1024 * 1024),
        cost_estimate=pl.CostEstimate(flops=2 * 256 * 256 * 19456, bytes_accessed=1 << 20, transcendentals=0),
    )(volts, pattern, owner_slot.reshape(1, stack_count))


def solution(mesh):
    return jax.shard_map(
        per_device,
        mesh=mesh,
        in_specs=(P(None, ("row", "col"), None), P(), P()),
        out_specs=P(("row", "col"), None, None),
        check_vma=False,
    )
```

```python
import functools

import jax
import jax.numpy as jnp
from jax import lax
from jax.experimental import pallas as pl
from jax.experimental.pallas import tpu as pltpu
from jax.sharding import PartitionSpec as P

GRID_COLUMNS = 128
CHAN = 2
TIME_SAMPLES = 256
DEPTH = 256
UNROLL = 8
MESH = pl.DeviceIdType.MESH


def iota(shape, dim):
    return lax.broadcasted_iota(jnp.int32, shape, dim)


def one_hot(condition):
    return jnp.where(condition, 1.0, 0.0).astype(jnp.bfloat16)


def dot(a, b, contract=((1,), (0,))):
    return lax.dot_general(a, b, (contract, ((), ())), preferred_element_type=jnp.float32)


def split3(x):
    high = x.astype(jnp.bfloat16)
    rest = x - high.astype(jnp.float32)
    middle = rest.astype(jnp.bfloat16)
    low = (rest - middle.astype(jnp.float32)).astype(jnp.bfloat16)
    return high, middle, low


def kernel(row_count, col_count, volts_hbm, pattern_hbm, owner_hbm, out_ref,
           volts_ref, pattern_ref, owner_ref, rhs_ref, lhs_ref, mask_ref, scale_ref, wanted_ref, sum_ref,
           send_ref, recv_ref, load_sems, send_sem, recv_sem):
    device_count = row_count * col_count
    grid_rows = pattern_ref.shape[0]
    samples = volts_ref.shape[1]
    unit = 2 * samples
    total = grid_rows * unit
    width = GRID_COLUMNS
    lanes = 2 * width
    stack_count = owner_ref.shape[1]
    mask_width = -(-stack_count // 128) * 128
    me = lax.axis_index("row") * col_count + lax.axis_index("col")

    def place(device):
        return (device // col_count, lax.rem(device, col_count))

    loads = [
        pltpu.make_async_copy(source, target, load_sems.at[n])
        for n, (source, target) in enumerate(
            ((pattern_hbm, pattern_ref), (owner_hbm, owner_ref), (volts_hbm, volts_ref)))
    ]
    for load in loads:
        load.start()

    barrier = pltpu.get_barrier_semaphore()

    def greet(step, carry):
        other = lax.rem(me + step, device_count)
        pl.semaphore_signal(barrier, inc=1, device_id=place(other), device_id_type=MESH)
        return carry

    lax.fori_loop(1, device_count, greet, 0, unroll=device_count <= 32)

    loads[0].wait()
    valid = jnp.where(pattern_ref[...] >= 0, 1.0, 0.0)
    flip_rows = one_hot(iota((grid_rows, grid_rows), 0) + iota((grid_rows, grid_rows), 1) == grid_rows - 1)
    more = mask_width - grid_rows
    widened = (
        jnp.concatenate([valid, jnp.zeros((grid_rows, more), valid.dtype)], axis=1),
        jnp.concatenate([valid, jnp.zeros((more, grid_rows), valid.dtype)], axis=0),
    )
    spread = one_hot(iota((grid_rows, total), 1) // unit == grid_rows - 1 - iota((grid_rows, total), 0))
    for sign, contract in enumerate((((1,), (0,)), ((1,), (1,)))):
        turned = dot(flip_rows, widened[sign].astype(jnp.bfloat16), contract)
        if sign == 0:
            unflipped = turned
        skewed = pltpu.roll(turned, mask_width - (grid_rows - 1), 1, stride=1, stride_axis=0)
        mask_ref[sign] = dot(skewed.T.astype(jnp.bfloat16)[:grid_rows], spread)

    rhs_ref[total:, :] = jnp.zeros((DEPTH, lanes), rhs_ref.dtype)
    sum_ref[:, stack_count - 8:, :] = jnp.zeros((4, 8, width), jnp.float32)

    loads[1].wait()
    loads[2].wait()
    store = rhs_ref.dtype
    for p in range(grid_rows):
        real = volts_ref[0, :, p * width:(p + 1) * width].astype(store)
        imag = volts_ref[1, :, p * width:(p + 1) * width].astype(store)
        start = p * unit
        rhs_ref[start:start + samples, :width] = real
        rhs_ref[start + samples:start + unit, :width] = imag
        rhs_ref[start:start + samples, width:] = -imag
        rhs_ref[start + samples:start + unit, width:] = real

    flip = one_hot(iota((width, width), 0) + iota((width, width), 1) == width - 1)
    for block in range(total // DEPTH):
        rows = rhs_ref[block * DEPTH:(block + 1) * DEPTH, :width].astype(jnp.bfloat16)
        lhs_ref[:, block * DEPTH:(block + 1) * DEPTH] = dot(flip, rows, ((1,), (1,))).astype(jnp.bfloat16)

    by_stack = pltpu.roll(unflipped, 0, 1, stride=1, stride_axis=0).T.astype(jnp.bfloat16)
    count = dot(by_stack, jnp.ones((grid_rows, lanes), jnp.bfloat16))[:stack_count]
    offsets = jnp.abs(iota((stack_count, lanes), 1) - (width - 1)).astype(jnp.float32)
    pairs = jnp.maximum(count * (width - offsets), 1.0)
    scale_ref[...] = 1.0 / jnp.sqrt(2.0 * TIME_SAMPLES * pairs)

    send_rows = device_count * 8
    owner = owner_ref[...]
    owner = jnp.concatenate([owner, owner, owner], axis=1)
    rows = iota((send_rows, 3 * stack_count), 0)
    slots = lax.rem(me + rows // 8, device_count) * 2 + rows // 4 % 2
    wanted_ref[...] = one_hot(slots == owner)

    unwrapped = iota((width, width), 1) >= iota((width, width), 0)

    def one_difference(depth, d, carry):
        left = lhs_ref[:, :depth].reshape(width // 16, 16, depth)
        masks = [
            jnp.broadcast_to(mask_ref[sign, pl.ds(d, 1), :depth], (16, depth)).astype(jnp.bfloat16)
            for sign in range(2)
        ]
        left = jnp.concatenate([(left * mask[None]).reshape(width, depth) for mask in masks], axis=0)
        right = rhs_ref[pl.ds(pl.multiple_of(d * unit, unit), depth), :].astype(jnp.bfloat16)
        gram = dot(left, right)
        for sign in range(2):
            k = grid_rows - 1 + d if sign == 0 else grid_rows - 1 - d
            for part in range(2):
                tile = gram[sign * width:(sign + 1) * width, part * width:(part + 1) * width]
                tile = pltpu.roll(tile, 0, 1, stride=1, stride_axis=0)
                first = jnp.where(unwrapped, tile, 0.0)
                second = jnp.where(unwrapped, 0.0, tile)
                sum_ref[2 * part, pl.ds(k, 1), :] = jnp.sum(first, axis=0, keepdims=True)
                sum_ref[2 * part + 1, pl.ds(k, 1), :] = jnp.sum(second, axis=0, keepdims=True)
        return carry

    per_block = DEPTH // unit
    for blocks in range(total // DEPTH, 0, -1):
        lax.fori_loop(
            grid_rows - blocks * per_block, grid_rows - (blocks - 1) * per_block,
            functools.partial(one_difference, blocks * DEPTH), 0, unroll=UNROLL)

    reverse = one_hot(iota((lanes, lanes), 0) + iota((lanes, lanes), 1) == lanes - 2)
    folded = [jnp.concatenate([sum_ref[2 * part], sum_ref[2 * part + 1]], axis=1) for part in range(2)]
    behind = jnp.concatenate([folded[part][:grid_rows] for part in range(2)], axis=0)
    behind = dot(jnp.concatenate(split3(behind), axis=0), reverse)
    behind = sum(behind[n * 2 * grid_rows:(n + 1) * 2 * grid_rows] for n in range(3))
    scale = scale_ref[...]
    real = jnp.concatenate([behind[:grid_rows], folded[0][grid_rows:]], axis=0) * scale
    imag = jnp.concatenate([-behind[grid_rows:], folded[1][grid_rows:]], axis=0) * scale
    stacked = jnp.concatenate([real, imag], axis=1)
    pieces = jnp.concatenate(split3(stacked), axis=0)

    def send(step, carry):
        pltpu.make_async_remote_copy(
            src_ref=send_ref.at[step], dst_ref=recv_ref.at[me], send_sem=send_sem, recv_sem=recv_sem,
            device_id=place(lax.rem(me + step, device_count)), device_id_type=MESH,
        ).start()
        return carry

    group = device_count // 4
    quarter = iota((group * 8, width), 0) % 4
    pl.semaphore_wait(barrier, device_count - 1)
    for first in range(0, device_count, group):
        picked = dot(wanted_ref[first * 8:(first + group) * 8, :], pieces)
        blocks = picked[:, 3 * width:]
        for m in range(3):
            blocks = jnp.where(quarter == m, picked[:, m * width:(m + 1) * width], blocks)
        send_ref[first:first + group] = blocks.reshape(group, 8, width)
        lax.fori_loop(max(first, 1), first + group, send, 0, unroll=device_count <= 32)
    recv_ref[me] = send_ref[0]
    others = pl.ds(0, device_count - 1)
    pltpu.make_async_copy(recv_ref.at[others], recv_ref.at[others], recv_sem).wait()
    half = device_count // CHAN
    for chan in range(CHAN):
        owned = jnp.sum(recv_ref[chan * half:(chan + 1) * half], axis=0)
        for slot in range(2):
            for part in range(2):
                line = slot * 4 + part * 2
                out_ref[slot, chan * 2 + part, :width] = owned[line]
                out_ref[slot, chan * 2 + part, width:] = owned[line + 1, :width - 1]
    pltpu.make_async_copy(send_ref.at[others], send_ref.at[others], send_sem).wait()


def per_device(volts, pattern, owner_slot):
    row_count = lax.axis_size("row")
    col_count = lax.axis_size("col")
    device_count = row_count * col_count
    grid_rows = pattern.shape[0]
    stack_count = owner_slot.shape[0]
    samples = volts.shape[1]
    total = grid_rows * 2 * samples
    store = jnp.bfloat16 if samples % 16 == 0 else jnp.float32
    vmem = pl.BlockSpec(memory_space=pltpu.VMEM)
    return pl.pallas_call(
        functools.partial(kernel, row_count, col_count),
        out_shape=jax.ShapeDtypeStruct(
            (stack_count // device_count, 2 * CHAN, 2 * GRID_COLUMNS - 1), jnp.float32),
        in_specs=[pl.BlockSpec(memory_space=pltpu.HBM)] * 3,
        out_specs=vmem,
        scratch_shapes=[
            pltpu.VMEM(volts.shape, volts.dtype),
            pltpu.VMEM(pattern.shape, pattern.dtype),
            pltpu.VMEM((1, stack_count), owner_slot.dtype),
            pltpu.VMEM((total + DEPTH, 2 * GRID_COLUMNS), store),
            pltpu.VMEM((GRID_COLUMNS, total), jnp.bfloat16),
            pltpu.VMEM((2, grid_rows, total), jnp.float32),
            pltpu.VMEM((stack_count, 2 * GRID_COLUMNS), jnp.float32),
            pltpu.VMEM((device_count * 8, 3 * stack_count), jnp.bfloat16),
            pltpu.VMEM((4, stack_count, GRID_COLUMNS), jnp.float32),
            pltpu.VMEM((device_count, 8, GRID_COLUMNS), jnp.float32),
            pltpu.VMEM((device_count, 8, GRID_COLUMNS), jnp.float32),
            pltpu.SemaphoreType.DMA((3,)),
            pltpu.SemaphoreType.DMA,
            pltpu.SemaphoreType.DMA,
        ],
        compiler_params=pltpu.CompilerParams(
            collective_id=0, has_side_effects=True, vmem_limit_bytes=55218 * 1024),
        cost_estimate=pl.CostEstimate(flops=2 * 256 * 256 * 19456, bytes_accessed=1 << 20, transcendentals=0),
    )(volts, pattern, owner_slot.reshape(1, stack_count))


def solution(mesh):
    return jax.shard_map(
        per_device,
        mesh=mesh,
        in_specs=(P(None, ("row", "col"), None), P(), P()),
        out_specs=P(("row", "col"), None, None),
        check_vma=False,
    )
```

```python
import functools

import jax
import jax.numpy as jnp
from jax import lax
from jax.experimental import pallas as pl
from jax.experimental.pallas import tpu as pltpu
from jax.sharding import PartitionSpec as P

GRID_COLUMNS = 128
CHAN = 2
TIME_SAMPLES = 256
DEPTH = 256
UNROLL = 8
MESH = pl.DeviceIdType.MESH


def iota(shape, dim):
    return lax.broadcasted_iota(jnp.int32, shape, dim)


def one_hot(condition):
    return jnp.where(condition, 1.0, 0.0).astype(jnp.bfloat16)


def dot(a, b, contract=((1,), (0,))):
    return lax.dot_general(a, b, (contract, ((), ())), preferred_element_type=jnp.float32)


def split3(x):
    high = x.astype(jnp.bfloat16)
    rest = x - high.astype(jnp.float32)
    middle = rest.astype(jnp.bfloat16)
    low = (rest - middle.astype(jnp.float32)).astype(jnp.bfloat16)
    return high, middle, low


def kernel(row_count, col_count, volts_hbm, pattern_hbm, owner_hbm, out_ref,
           volts_ref, pattern_ref, owner_ref, rhs_ref, lhs_ref, mask_ref, scale_ref, wanted_ref, sum_ref,
           send_ref, recv_ref, load_sems, send_sem, recv_sem):
    device_count = row_count * col_count
    grid_rows = pattern_ref.shape[0]
    samples = volts_ref.shape[1]
    unit = 2 * samples
    total = grid_rows * unit
    width = GRID_COLUMNS
    lanes = 2 * width
    stack_count = owner_ref.shape[1]
    mask_width = -(-stack_count // 128) * 128
    me = lax.axis_index("row") * col_count + lax.axis_index("col")

    def place(device):
        return (device // col_count, lax.rem(device, col_count))

    loads = [
        pltpu.make_async_copy(source, target, load_sems.at[n])
        for n, (source, target) in enumerate(
            ((pattern_hbm, pattern_ref), (owner_hbm, owner_ref), (volts_hbm, volts_ref)))
    ]
    for load in loads:
        load.start()

    barrier = pltpu.get_barrier_semaphore()

    def greet(step, carry):
        other = lax.rem(me + step, device_count)
        pl.semaphore_signal(barrier, inc=1, device_id=place(other), device_id_type=MESH)
        return carry

    lax.fori_loop(1, device_count, greet, 0, unroll=device_count <= 32)

    loads[0].wait()
    valid = jnp.where(pattern_ref[...] >= 0, 1.0, 0.0)
    flip_rows = one_hot(iota((grid_rows, grid_rows), 0) + iota((grid_rows, grid_rows), 1) == grid_rows - 1)
    more = mask_width - grid_rows
    widened = (
        jnp.concatenate([valid, jnp.zeros((grid_rows, more), valid.dtype)], axis=1),
        jnp.concatenate([valid, jnp.zeros((more, grid_rows), valid.dtype)], axis=0),
    )
    spread = one_hot(iota((grid_rows, total), 1) // unit == grid_rows - 1 - iota((grid_rows, total), 0))
    for sign, contract in enumerate((((1,), (0,)), ((1,), (1,)))):
        turned = dot(flip_rows, widened[sign].astype(jnp.bfloat16), contract)
        if sign == 0:
            unflipped = turned
        skewed = pltpu.roll(turned, mask_width - (grid_rows - 1), 1, stride=1, stride_axis=0)
        mask_ref[sign] = dot(skewed.T.astype(jnp.bfloat16)[:grid_rows], spread)

    rhs_ref[total:, :] = jnp.zeros((DEPTH, lanes), rhs_ref.dtype)
    sum_ref[:, stack_count - 8:, :] = jnp.zeros((4, 8, width), jnp.float32)
    sum_ref[:, grid_rows - 8:grid_rows, :] = jnp.zeros((4, 8, width), jnp.float32)

    loads[1].wait()
    loads[2].wait()
    store = rhs_ref.dtype
    for p in range(grid_rows):
        real = volts_ref[0, :, p * width:(p + 1) * width].astype(store)
        imag = volts_ref[1, :, p * width:(p + 1) * width].astype(store)
        start = p * unit
        rhs_ref[start:start + samples, :width] = real
        rhs_ref[start + samples:start + unit, :width] = imag
        rhs_ref[start:start + samples, width:] = -imag
        rhs_ref[start + samples:start + unit, width:] = real

    flip = one_hot(iota((width, width), 0) + iota((width, width), 1) == width - 1)
    for block in range(total // DEPTH):
        rows = rhs_ref[block * DEPTH:(block + 1) * DEPTH, :width].astype(jnp.bfloat16)
        lhs_ref[:, block * DEPTH:(block + 1) * DEPTH] = dot(flip, rows, ((1,), (1,))).astype(jnp.bfloat16)

    by_stack = pltpu.roll(unflipped, 0, 1, stride=1, stride_axis=0).T.astype(jnp.bfloat16)
    count = dot(by_stack, jnp.ones((grid_rows, lanes), jnp.bfloat16))[:stack_count]
    offsets = jnp.abs(iota((stack_count, lanes), 1) - (width - 1)).astype(jnp.float32)
    pairs = jnp.maximum(count * (width - offsets), 1.0)
    scale_ref[...] = 1.0 / jnp.sqrt(2.0 * TIME_SAMPLES * pairs)

    send_rows = device_count * 8
    owner = owner_ref[...]
    owner = jnp.concatenate([owner, owner, owner], axis=1)
    rows = iota((send_rows, 3 * stack_count), 0)
    slots = lax.rem(me + rows // 8, device_count) * 2 + rows // 4 % 2
    wanted_ref[...] = one_hot(slots == owner)

    unwrapped = iota((width, width), 1) >= iota((width, width), 0)

    def one_difference(depth, d, carry):
        left = lhs_ref[:, :depth].reshape(width // 16, 16, depth)
        masks = [
            jnp.broadcast_to(mask_ref[sign, pl.ds(d, 1), :depth], (16, depth)).astype(jnp.bfloat16)
            for sign in range(2)
        ]
        left = jnp.concatenate([(left * mask[None]).reshape(width, depth) for mask in masks], axis=0)
        right = rhs_ref[pl.ds(pl.multiple_of(d * unit, unit), depth), :].astype(jnp.bfloat16)
        gram = dot(left, right)
        for sign in range(2):
            k = grid_rows - 1 + d if sign == 0 else grid_rows - 1 - d
            for part in range(2):
                tile = gram[sign * width:(sign + 1) * width, part * width:(part + 1) * width]
                tile = pltpu.roll(tile, 0, 1, stride=1, stride_axis=0)
                first = jnp.where(unwrapped, tile, 0.0)
                second = jnp.where(unwrapped, 0.0, tile)
                sum_ref[2 * part, pl.ds(k, 1), :] = jnp.sum(first, axis=0, keepdims=True)
                sum_ref[2 * part + 1, pl.ds(k, 1), :] = jnp.sum(second, axis=0, keepdims=True)
        return carry

    per_block = DEPTH // unit
    for blocks in range(total // DEPTH, 0, -1):
        begin = max(1, grid_rows - blocks * per_block)
        end = grid_rows - (blocks - 1) * per_block
        lax.fori_loop(
            begin, end, functools.partial(one_difference, blocks * DEPTH), 0,
            unroll=end - begin if end - begin <= UNROLL else 1)

    reverse = one_hot(iota((lanes, lanes), 0) + iota((lanes, lanes), 1) == lanes - 2)
    folded = [jnp.concatenate([sum_ref[2 * part], sum_ref[2 * part + 1]], axis=1) for part in range(2)]
    behind = jnp.concatenate([folded[part][:grid_rows] for part in range(2)], axis=0)
    behind = dot(jnp.concatenate(split3(behind), axis=0), reverse)
    behind = sum(behind[n * 2 * grid_rows:(n + 1) * 2 * grid_rows] for n in range(3))
    scale = scale_ref[...]
    real = jnp.concatenate([behind[:grid_rows], folded[0][grid_rows:]], axis=0) * scale
    imag = jnp.concatenate([-behind[grid_rows:], folded[1][grid_rows:]], axis=0) * scale
    stacked = jnp.concatenate([real, imag], axis=1)
    pieces = jnp.concatenate(split3(stacked), axis=0)

    def send(step, carry):
        pltpu.make_async_remote_copy(
            src_ref=send_ref.at[step], dst_ref=recv_ref.at[me], send_sem=send_sem, recv_sem=recv_sem,
            device_id=place(lax.rem(me + step, device_count)), device_id_type=MESH,
        ).start()
        return carry

    group = device_count // 4
    quarter = iota((group * 8, width), 0) % 4
    pl.semaphore_wait(barrier, device_count - 1)
    for first in range(0, device_count, group):
        picked = dot(wanted_ref[first * 8:(first + group) * 8, :], pieces)
        blocks = picked[:, 3 * width:]
        for m in range(3):
            blocks = jnp.where(quarter == m, picked[:, m * width:(m + 1) * width], blocks)
        send_ref[first:first + group] = blocks.reshape(group, 8, width)
        lax.fori_loop(max(first, 1), first + group, send, 0, unroll=device_count <= 32)
    recv_ref[me] = send_ref[0]
    others = pl.ds(0, device_count - 1)
    pltpu.make_async_copy(recv_ref.at[others], recv_ref.at[others], recv_sem).wait()
    half = device_count // CHAN
    for chan in range(CHAN):
        owned = jnp.sum(recv_ref[chan * half:(chan + 1) * half], axis=0)
        for slot in range(2):
            for part in range(2):
                line = slot * 4 + part * 2
                out_ref[slot, chan * 2 + part, :width] = owned[line]
                out_ref[slot, chan * 2 + part, width:] = owned[line + 1, :width - 1]
    pltpu.make_async_copy(send_ref.at[others], send_ref.at[others], send_sem).wait()


def per_device(volts, pattern, owner_slot):
    row_count = lax.axis_size("row")
    col_count = lax.axis_size("col")
    device_count = row_count * col_count
    grid_rows = pattern.shape[0]
    stack_count = owner_slot.shape[0]
    samples = volts.shape[1]
    total = grid_rows * 2 * samples
    store = jnp.bfloat16 if samples % 16 == 0 else jnp.float32
    vmem = pl.BlockSpec(memory_space=pltpu.VMEM)
    return pl.pallas_call(
        functools.partial(kernel, row_count, col_count),
        out_shape=jax.ShapeDtypeStruct(
            (stack_count // device_count, 2 * CHAN, 2 * GRID_COLUMNS - 1), jnp.float32),
        in_specs=[pl.BlockSpec(memory_space=pltpu.HBM)] * 3,
        out_specs=vmem,
        scratch_shapes=[
            pltpu.VMEM(volts.shape, volts.dtype),
            pltpu.VMEM(pattern.shape, pattern.dtype),
            pltpu.VMEM((1, stack_count), owner_slot.dtype),
            pltpu.VMEM((total + DEPTH, 2 * GRID_COLUMNS), store),
            pltpu.VMEM((GRID_COLUMNS, total), jnp.bfloat16),
            pltpu.VMEM((2, grid_rows, total), jnp.float32),
            pltpu.VMEM((stack_count, 2 * GRID_COLUMNS), jnp.float32),
            pltpu.VMEM((device_count * 8, 3 * stack_count), jnp.bfloat16),
            pltpu.VMEM((4, stack_count, GRID_COLUMNS), jnp.float32),
            pltpu.VMEM((device_count, 8, GRID_COLUMNS), jnp.float32),
            pltpu.VMEM((device_count, 8, GRID_COLUMNS), jnp.float32),
            pltpu.SemaphoreType.DMA((3,)),
            pltpu.SemaphoreType.DMA,
            pltpu.SemaphoreType.DMA,
        ],
        compiler_params=pltpu.CompilerParams(
            collective_id=0, has_side_effects=True, vmem_limit_bytes=55218 * 1024),
        cost_estimate=pl.CostEstimate(flops=2 * 256 * 256 * 19456, bytes_accessed=1 << 20, transcendentals=0),
    )(volts, pattern, owner_slot.reshape(1, stack_count))


def solution(mesh):
    return jax.shard_map(
        per_device,
        mesh=mesh,
        in_specs=(P(None, ("row", "col"), None), P(), P()),
        out_specs=P(("row", "col"), None, None),
        check_vma=False,
    )
```
